32 devices in a mesh: row: 8 (over z, x), pair: 4 (over y, core).
Axes of the slice: x: 2, y: 2, z: 4, core: 2. Of those that a mesh axis runs over, the one named last changes fastest.
Arguments:
- matrix: float32 [1536, 2048], P('row', 'pair'), may hold values from -50 to 50
- seating: int32 [8], replicated, may hold values from 0 to 7, each once
Outputs:
- rotated: float32 [1536, 2048], P('row', 'pair')
The draws below stay inside these ranges and needn't reach their ends.
All inputs are finite; a program needn't handle non-finite values.
Results may differ from the reference program's by a relative error of at most 0.0003.
Values sent between devices are 32-bit elements; how exact they have to be, the bound alone decides.
A program may use at most 64 MiB of HBM per device.

```python
import jax
import jax.numpy as jnp
from jax import lax

B = 256
STEPS = 4
INNER = 4
NBLK = 8
COLS = 2048
ROWS = 1536


def draw_matrix(key, part):
    key = jax.random.fold_in(key, 11)
    first, second, third = jax.random.split(key, 3)
    base = jnp.clip(jax.random.normal(first, (ROWS, COLS), jnp.float32), -5.0, 5.0)
    row_scales = jnp.exp(jax.random.uniform(second, (ROWS, 1), jnp.float32) * jnp.log(10.0))
    column_scales = jnp.exp(jax.random.uniform(third, (1, COLS), jnp.float32) * jnp.log(10.0))
    return base * row_scales * column_scales / 10.0


def setup_inputs(seed: int = 0) -> dict:
    streams_of = jax.random.split(jax.random.key(seed), 3)
    return {
        "matrix": draw_matrix(jax.random.fold_in(streams_of[2], 71), 0),
        "seating": jax.random.permutation(streams_of[1], NBLK).astype(jnp.int32),
    }


def columns_turn(block, cosines, sines):
    left = block[:, :B]
    right = block[:, B:]
    return jnp.concatenate([cosines * left - sines * right, sines * left + cosines * right], axis=1)

def rows_turn(block, cosines, sines):
    left = block[:B]
    right = block[B:]
    return jnp.concatenate([cosines[:, None] * left - sines[:, None] * right, sines[:, None] * left + cosines[:, None] * right], axis=0)

def roll_lower(block, axis_number):
    if axis_number == 1:
        return jnp.concatenate([block[:, :B], jnp.roll(block[:, B:], -1, axis=1)], axis=1)
    return jnp.concatenate([block[:B], jnp.roll(block[B:], -1, axis=0)], axis=0)

def solve_pair(gram):
    rotation = jnp.eye(2 * B, dtype=jnp.float32)
    for sweep in range(INNER):
        whole_diag = jnp.diagonal(gram)
        upper_diag = whole_diag[:B]
        lower_diag = whole_diag[B:]
        coupling = jnp.diagonal(gram[:B, B:])
        differ = lower_diag - upper_diag
        signs = jnp.where(differ >= 0.0, 1.0, -1.0).astype(jnp.float32)
        denom = jnp.abs(differ) + jnp.sqrt(differ * differ + 4.0 * coupling * coupling + 1e-12 * (upper_diag + lower_diag) ** 2)
        tangent = 2.0 * signs * coupling / denom
        cosines = 1.0 / jnp.sqrt(1.0 + tangent * tangent)
        sines = tangent * cosines
        gram = rows_turn(columns_turn(gram, cosines, sines), cosines, sines)
        rotation = columns_turn(rotation, cosines, sines)
        gram = roll_lower(roll_lower(gram, 1), 0)
        rotation = roll_lower(rotation, 1)
    rotation = jnp.concatenate([rotation[:, :B], jnp.roll(rotation[:, B:], INNER, axis=1)], axis=1)
    return (rotation, gram)

def rotate_pair(blocks):
    joined = jnp.concatenate([blocks[0], blocks[1]], axis=1)
    gram = jnp.dot(joined.T, joined, precision=lax.Precision.HIGHEST, preferred_element_type=jnp.float32)
    rotation, turned = solve_pair(gram)
    result = jnp.dot(joined, rotation, precision=lax.Precision.HIGHEST, preferred_element_type=jnp.float32)
    return (result[:, :B], result[:, B:])

def reference(matrix, seating):
    tables = NBLK // 2
    blocks = matrix.reshape(ROWS, NBLK, B)
    seated = jnp.transpose(blocks[:, seating.astype(jnp.int32), :], (1, 0, 2))
    upper = seated[0::2]
    lower = seated[1::2]
    for step in range(STEPS):
        upper, lower = lax.map(rotate_pair, (upper, lower))
        new_upper = jnp.concatenate([upper[0:1], lower[0:1], upper[1:tables - 1]], axis=0)
        new_lower = jnp.concatenate([lower[1:], upper[tables - 1:]], axis=0)
        upper, lower = (new_upper, new_lower)
    stacked = jnp.stack([upper, lower], axis=1)
    return jnp.transpose(stacked, (2, 0, 1, 3)).reshape(ROWS, COLS)
```

```python
import jax
import jax.numpy as jnp
from jax import lax
from jax.sharding import PartitionSpec as P

B = 256
STEPS = 4
INNER = 4


def shifted(block, axis, distance):
    devices = range(lax.axis_size(axis))
    route = [(i - distance, i) for i in devices if i - distance in devices]
    return lax.ppermute(block, axis, route)


def ahead(values, distance):
    return jnp.roll(values, -distance, axis=-1) if distance else values


def band_sums(upper, lower):
    rows = []
    for o in range(INNER):
        u, l = ahead(upper, o), ahead(lower, o)
        rows += [upper * u, lower * l, upper * l]
        if o:
            rows += [lower * u]
    return jnp.stack([jnp.sum(row, axis=0) for row in rows])


def solve_bands(bands):
    uu, ll, ul, lu = {}, {}, {}, {}
    at = 0
    for o in range(INNER):
        uu[o], ll[o], ul[o] = bands[at], bands[at + 1], bands[at + 2]
        at += 3
        if o:
            lu[o] = bands[at]
            at += 1
    turns = []
    for sweep in range(INNER):
        differ = ll[0] - uu[0]
        coupling = ul[0]
        signs = jnp.where(differ >= 0.0, 1.0, -1.0).astype(jnp.float32)
        total = uu[0] + ll[0]
        denom = jnp.abs(differ) + jnp.sqrt(
            differ * differ + 4.0 * coupling * coupling + 1e-12 * (total * total)
        )
        tangent = 2.0 * signs * coupling / denom
        c = 1.0 / jnp.sqrt(1.0 + tangent * tangent)
        s = tangent * c
        turns.append((c, s))
        reach = INNER - 1 - sweep
        if reach == 0:
            break
        new_uu, new_ll, new_ul, new_lu = {}, {}, {}, {}
        for o in range(reach + 1):
            cj, sj = ahead(c, o), ahead(s, o)
            a, b, d = uu[o], ul[o], ll[o]
            e = lu[o] if o else ul[0]
            top_u, top_l = c * a - s * e, c * b - s * d
            low_u, low_l = s * a + c * e, s * b + c * d
            new_ul[o] = sj * top_u + cj * top_l
            if o < reach:
                new_uu[o] = cj * top_u - sj * top_l
                new_ll[o] = sj * low_u + cj * low_l
                if o:
                    new_lu[o] = cj * low_u - sj * low_l
        uu = new_uu
        ll = {o: ahead(new_ll[o], 1) for o in new_ll}
        ul = {o: new_ul[o + 1] for o in range(reach)}
        lu = {o: ahead(new_lu[o - 1] if o > 1 else new_ul[0], 1) for o in range(1, reach)}
    return turns


def turn(upper, lower, turns):
    for k, (c, s) in enumerate(turns):
        upper, lower = c * upper - s * lower, s * upper + c * lower
        if k < INNER - 1:
            lower = ahead(lower, 1)
    return upper, ahead(lower, 1 - INNER)


def local(matrix, seating):
    height = matrix.shape[0]
    place = lax.axis_index("pair")
    tables = lax.axis_size("pair")
    wanted = lax.dynamic_slice(seating, (2 * place,), (2,))
    piece = lax.all_gather(matrix, "pair", axis=1, tiled=True)
    count = piece.shape[1] // B
    shaped = piece.reshape(height, count, B)
    labels = jnp.arange(count, dtype=jnp.int32)
    upper = jnp.sum(jnp.where((labels == wanted[0])[None, :, None], shaped, 0.0), axis=1)
    lower = jnp.sum(jnp.where((labels == wanted[1])[None, :, None], shaped, 0.0), axis=1)
    first_table = place == 0
    last_table = place == tables - 1
    for step in range(STEPS):
        bands = lax.psum(band_sums(upper, lower), "row")
        upper, lower = turn(upper, lower, solve_bands(bands))
        sent_up = jnp.where(first_table, lower, upper)
        arrived_up = shifted(sent_up, "pair", 1)
        arrived_down = shifted(lower, "pair", -1)
        new_upper = jnp.where(first_table, upper, arrived_up)
        new_lower = jnp.where(last_table, upper, arrived_down)
        upper, lower = (new_upper, new_lower)
    return jnp.concatenate([upper, lower], axis=1)


def solution(mesh):
    in_specs = (P("row", "pair"), P())
    out_specs = P("row", "pair")
    return jax.shard_map(local, mesh=mesh, in_specs=in_specs, out_specs=out_specs, check_vma=False)
```

```python
import functools

import jax
import jax.numpy as jnp
from jax import lax
from jax.experimental import pallas as pl
from jax.experimental.pallas import tpu as pltpu
from jax.sharding import PartitionSpec as P

B = 256
STEPS = 4
INNER = 4
TILE = 8
CHUNKS = 2
BANDS = 4 * INNER
MESH = pl.DeviceIdType.MESH


def ahead(values, distance):
    shift = (-distance) % B
    return pltpu.roll(values, shift, axis=1) if shift else values


def band_products(upper, lower):
    products = []
    for o in range(INNER):
        u, l = ahead(upper, o), ahead(lower, o)
        products += [upper * u, lower * l, upper * l]
        if o:
            products.append(lower * u)
    return products


def solve_bands(bands):
    uu, ll, ul, lu = {}, {}, {}, {}
    at = 0
    for o in range(INNER):
        uu[o], ll[o], ul[o] = bands[at], bands[at + 1], bands[at + 2]
        at += 3
        if o:
            lu[o] = bands[at]
            at += 1
    turns = []
    for sweep in range(INNER):
        differ = ll[0] - uu[0]
        coupling = ul[0]
        total = uu[0] + ll[0]
        signs = jnp.where(differ >= 0.0, 1.0, -1.0)
        denom = jnp.abs(differ) + jnp.sqrt(
            differ * differ + 4.0 * coupling * coupling + 1e-12 * (total * total)
        )
        tangent = 2.0 * signs * coupling / denom
        c = 1.0 / jnp.sqrt(1.0 + tangent * tangent)
        s = tangent * c
        turns.append((c, s))
        reach = INNER - 1 - sweep
        if reach == 0:
            break
        new_uu, new_ll, new_ul, new_lu = {}, {}, {}, {}
        for o in range(reach + 1):
            cj, sj = ahead(c, o), ahead(s, o)
            a, b, d = uu[o], ul[o], ll[o]
            e = lu[o] if o else ul[0]
            top_u, top_l = c * a - s * e, c * b - s * d
            low_u, low_l = s * a + c * e, s * b + c * d
            new_ul[o] = sj * top_u + cj * top_l
            if o < reach:
                new_uu[o] = cj * top_u - sj * top_l
                new_ll[o] = sj * low_u + cj * low_l
                if o:
                    new_lu[o] = cj * low_u - sj * low_l
        uu = new_uu
        ll = {o: ahead(new_ll[o], 1) for o in new_ll}
        ul = {o: new_ul[o + 1] for o in range(reach)}
        lu = {o: ahead(new_lu[o - 1] if o > 1 else new_ul[0], 1) for o in range(1, reach)}
    return turns


def turn(upper, lower, turns):
    for k, (c, s) in enumerate(turns):
        upper, lower = c * upper - s * lower, s * upper + c * lower
        if k < INNER - 1:
            lower = ahead(lower, 1)
    return upper, ahead(lower, 1 - INNER)


def kernel(
    nrow, npair, seat_ref, m_ref, out_ref, g, x, r, part,
    g_send, f_send, g_recv, p_send, p_recv, m_send, m_recv, own_sem,
):
    me = lax.axis_index("row")
    place = lax.axis_index("pair")
    height = m_ref.shape[0]
    chunk = height // CHUNKS
    core = lax.rem(place, 2)
    across = lax.div(place, 2)
    nacross = npair // 2
    sibling = 2 * across + 1 - core
    has_next = place < npair - 1
    has_prev = place > 0

    barrier = pltpu.get_barrier_semaphore()
    for d in range(1, npair):
        pl.semaphore_signal(
            barrier, inc=1, device_id=(me, lax.rem(place + d, npair)), device_id_type=MESH
        )
    for d in range(1, nrow):
        pl.semaphore_signal(
            barrier, inc=1, device_id=(lax.rem(me + d, nrow), place), device_id_type=MESH
        )
    pl.semaphore_wait(barrier, npair + nrow - 2)

    def remote(src, dst, send, recv, device):
        return pltpu.make_async_remote_copy(
            src_ref=src, dst_ref=dst, send_sem=send, recv_sem=recv,
            device_id=device, device_id_type=MESH,
        )

    def columns(b):
        return m_ref.at[:, pl.ds(b * B, B)]

    def direct(d, b):
        target = sibling if d == 0 else 2 * lax.rem(across + d, nacross) + core
        slot = 2 * place + b
        return remote(columns(b), g.at[slot], g_send.at[d, b], g_recv.at[slot], (me, target))

    def forward(d, b):
        slot = 2 * (2 * lax.rem(across + d, nacross) + core) + b
        return remote(g.at[slot], g.at[slot], f_send.at[d, b], g_recv.at[slot], (me, sibling))

    for b in range(2):
        for d in range(1, nacross):
            direct(d, b).start()
    for b in range(2):
        direct(0, b).start()
    own = [
        pltpu.make_async_copy(columns(b), g.at[2 * place + b], own_sem.at[b]) for b in range(2)
    ]
    for copy in own:
        copy.start()
    for b in range(2):
        for d in range(1, nacross):
            forward(d, b).wait_recv()
            forward(d, b).start()
    for copy in own:
        copy.wait()
    for b in range(2):
        for d in range(nacross):
            slot = 2 * (2 * lax.rem(across + d, nacross) + 1 - core) + b
            remote(
                g.at[slot], g.at[slot], f_send.at[0, b], g_recv.at[slot], (me, sibling)
            ).wait_recv()

    first = seat_ref[2 * place]
    second = seat_ref[2 * place + 1]

    @pl.loop(0, height // TILE)
    def seat(t):
        rows = pl.ds(t * TILE, TILE)
        x[0, 0, rows, :] = g[first, rows, :]
        x[0, 1, rows, :] = g[second, rows, :]

    def partial_copy(s, d):
        return remote(
            part.at[s, me], part.at[s, me], p_send.at[s, d], p_recv.at[s, me],
            (lax.rem(me + d, nrow), place),
        )

    def move(s, way, c):
        rows = pl.ds(c * chunk, chunk)
        if way == 0:
            src = r.at[s, jnp.where(has_prev, 0, 1), rows]
            target = lax.rem(place + 1, npair)
        else:
            src = r.at[s, 1, rows]
            target = lax.rem(place + npair - 1, npair)
        return remote(
            src, x.at[s + 1, way, rows], m_send.at[s, way, c], m_recv.at[s, way, c], (me, target)
        )

    def arrived(s, c):
        @pl.when(has_prev)
        def _():
            move(s, 0, c).wait_recv()

        @pl.when(has_next)
        def _():
            move(s, 1, c).wait_recv()

    kept = jnp.where(has_prev, jnp.where(has_next, 2, 1), 0)

    @pl.loop(0, STEPS)
    def step(s):
        sums = tuple(jnp.zeros((TILE, B), jnp.float32) for _ in range(BANDS - 1))
        for c in range(CHUNKS):
            @pl.when(s > 0)
            def _():
                arrived(s - 1, c)

            def add(t, totals):
                rows = pl.ds(c * chunk + t * TILE, TILE)
                products = band_products(x[s, 0, rows, :], x[s, 1, rows, :])
                return tuple(a + b for a, b in zip(totals, products))

            sums = lax.fori_loop(0, chunk // TILE, add, sums)
        for k in range(BANDS - 1):
            part[s, me, k:k + 1, :] = jnp.sum(sums[k], axis=0, keepdims=True)
        part[s, me, BANDS - 1:BANDS, :] = jnp.zeros((1, B), jnp.float32)
        for d in range(1, nrow):
            partial_copy(s, d).start()
        for d in range(1, nrow):
            source = lax.rem(me + d, nrow)
            remote(
                part.at[s, source], part.at[s, source], p_send.at[s, d], p_recv.at[s, source],
                (source, place),
            ).wait_recv()
        whole = part[s, 0]
        for k in range(1, nrow):
            whole = whole + part[s, k]
        bands = [jnp.broadcast_to(whole[k:k + 1, :], (TILE, B)) for k in range(BANDS - 1)]
        turns = solve_bands(bands)
        for c in range(CHUNKS):
            @pl.loop(0, chunk // TILE)
            def rotate(t):
                rows = pl.ds(c * chunk + t * TILE, TILE)
                upper, lower = turn(x[s, 0, rows, :], x[s, 1, rows, :], turns)
                r[s, 0, rows, :] = upper
                r[s, 1, rows, :] = lower
                x[s + 1, kept, rows, :] = upper

            @pl.when(has_next)
            def _():
                move(s, 0, c).start()

            @pl.when(has_prev)
            def _():
                move(s, 1, c).start()

    for c in range(CHUNKS):
        arrived(STEPS - 1, c)

        @pl.loop(0, chunk // TILE)
        def hand_out(t):
            rows = pl.ds(c * chunk + t * TILE, TILE)
            out_ref[rows, 0:B] = x[STEPS, 0, rows, :]
            out_ref[rows, B:2 * B] = x[STEPS, 1, rows, :]

    for b in range(2):
        for d in range(nacross):
            direct(d, b).wait_send()
            if d:
                forward(d, b).wait_send()

    @pl.loop(0, STEPS)
    def drain(s):
        for d in range(1, nrow):
            partial_copy(s, d).wait_send()
        for c in range(CHUNKS):
            @pl.when(has_next)
            def _():
                move(s, 0, c).wait_send()

            @pl.when(has_prev)
            def _():
                move(s, 1, c).wait_send()


def local(nrow, npair, matrix, seating):
    height = matrix.shape[0]
    nacross = npair // 2
    dma = pltpu.SemaphoreType.DMA
    return pl.pallas_call(
        functools.partial(kernel, nrow, npair),
        out_shape=jax.ShapeDtypeStruct(matrix.shape, jnp.float32),
        in_specs=[
            pl.BlockSpec(memory_space=pltpu.SMEM),
            pl.BlockSpec(memory_space=pltpu.VMEM),
        ],
        out_specs=pl.BlockSpec(memory_space=pltpu.VMEM),
        scratch_shapes=[
            pltpu.VMEM((2 * npair, height, B), jnp.float32),
            pltpu.VMEM((STEPS + 1, 3, height, B), jnp.float32),
            pltpu.VMEM((STEPS, 2, height, B), jnp.float32),
            pltpu.VMEM((STEPS, nrow, BANDS, B), jnp.float32),
            dma((nacross, 2)),
            dma((nacross, 2)),
            dma((2 * npair,)),
            dma((STEPS, nrow)),
            dma((STEPS, nrow)),
            dma((STEPS, 2, CHUNKS)),
            dma((STEPS, 2, CHUNKS)),
            dma((2,)),
        ],
        compiler_params=pltpu.CompilerParams(
            collective_id=0, has_side_effects=True, vmem_limit_bytes=32 * 1024 * 1024
        ),
    )(seating, matrix)


def solution(mesh):
    sizes = dict(mesh.shape)
    return jax.shard_map(
        functools.partial(local, sizes["row"], sizes["pair"]),
        mesh=mesh, in_specs=(P("row", "pair"), P()), out_specs=P("row", "pair"), check_vma=False,
    )
```

```python
import functools

import jax
import jax.numpy as jnp
from jax import lax
from jax.experimental import pallas as pl
from jax.experimental.pallas import tpu as pltpu
from jax.sharding import PartitionSpec as P

B = 256
STEPS = 4
INNER = 4
TILE = 8
GROUP = 4
CHUNKS = 2
BANDS = 4 * INNER
MESH = pl.DeviceIdType.MESH


def ahead(values, distance):
    shift = (-distance) % B
    return pltpu.roll(values, shift, axis=1) if shift else values


def band_products(upper, lower):
    products = []
    for o in range(INNER):
        u, l = ahead(upper, o), ahead(lower, o)
        products += [upper * u, lower * l, upper * l]
        if o:
            products.append(lower * u)
    return products


def solve_bands(bands):
    uu, ll, ul, lu = {}, {}, {}, {}
    at = 0
    for o in range(INNER):
        uu[o], ll[o], ul[o] = bands[at], bands[at + 1], bands[at + 2]
        at += 3
        if o:
            lu[o] = bands[at]
            at += 1
    turns = []
    for sweep in range(INNER):
        differ = ll[0] - uu[0]
        coupling = ul[0]
        total = uu[0] + ll[0]
        signs = jnp.where(differ >= 0.0, 1.0, -1.0)
        denom = jnp.abs(differ) + jnp.sqrt(
            differ * differ + 4.0 * coupling * coupling + 1e-12 * (total * total)
        )
        tangent = 2.0 * signs * coupling / denom
        c = lax.rsqrt(1.0 + tangent * tangent)
        s = tangent * c
        turns.append((c, s))
        reach = INNER - 1 - sweep
        if reach == 0:
            break
        new_uu, new_ll, new_ul, new_lu = {}, {}, {}, {}
        for o in range(reach + 1):
            cj, sj = ahead(c, o), ahead(s, o)
            a, b, d = uu[o], ul[o], ll[o]
            e = lu[o] if o else ul[0]
            top_u, top_l = c * a - s * e, c * b - s * d
            low_u, low_l = s * a + c * e, s * b + c * d
            new_ul[o] = sj * top_u + cj * top_l
            if o < reach:
                new_uu[o] = cj * top_u - sj * top_l
                new_ll[o] = sj * low_u + cj * low_l
                if o:
                    new_lu[o] = cj * low_u - sj * low_l
        uu = new_uu
        ll = {o: ahead(new_ll[o], 1) for o in new_ll}
        ul = {o: new_ul[o + 1] for o in range(reach)}
        lu = {o: ahead(new_lu[o - 1] if o > 1 else new_ul[0], 1) for o in range(1, reach)}
    return turns


def turn(pairs, turns):
    for k, (c, s) in enumerate(turns):
        pairs = [(c * u - s * l, s * u + c * l) for u, l in pairs]
        distance = 1 if k < INNER - 1 else 1 - INNER
        pairs = [(u, ahead(l, distance)) for u, l in pairs]
    return pairs


def kernel(
    nrow, npair, seating_ref, m_ref, out_ref, seat_ref, g, x, r, part,
    g_send, f_send, g_recv, p_send, p_recv, m_send, m_recv, own_sem, seat_sem,
):
    me = lax.axis_index("row")
    place = lax.axis_index("pair")
    height = m_ref.shape[0]
    chunk = height // CHUNKS
    core = lax.rem(place, 2)
    across = lax.div(place, 2)
    nacross = npair // 2
    sibling = 2 * across + 1 - core
    has_next = place < npair - 1
    has_prev = place > 0

    barrier = pltpu.get_barrier_semaphore()
    for d in range(1, npair):
        pl.semaphore_signal(
            barrier, inc=1, device_id=(me, lax.rem(place + d, npair)), device_id_type=MESH
        )
    for d in range(1, nrow):
        pl.semaphore_signal(
            barrier, inc=1, device_id=(lax.rem(me + d, nrow), place), device_id_type=MESH
        )
    pl.semaphore_wait(barrier, npair + nrow - 2)

    def remote(src, dst, send, recv, device):
        return pltpu.make_async_remote_copy(
            src_ref=src, dst_ref=dst, send_sem=send, recv_sem=recv,
            device_id=device, device_id_type=MESH,
        )

    def columns(b):
        return m_ref.at[:, pl.ds(b * B, B)]

    def direct(d, b):
        target = sibling if d == 0 else 2 * lax.rem(across + d, nacross) + core
        slot = 2 * place + b
        return remote(columns(b), g.at[slot], g_send.at[d, b], g_recv.at[slot], (me, target))

    def forward(d, b):
        slot = 2 * (2 * lax.rem(across + d, nacross) + core) + b
        return remote(g.at[slot], g.at[slot], f_send.at[d, b], g_recv.at[slot], (me, sibling))

    for b in range(2):
        for d in range(1, nacross):
            direct(d, b).start()
    for b in range(2):
        direct(0, b).start()
    seats = pltpu.make_async_copy(seating_ref, seat_ref, seat_sem)
    seats.start()
    own = [
        pltpu.make_async_copy(columns(b), g.at[2 * place + b], own_sem.at[b]) for b in range(2)
    ]
    for copy in own:
        copy.start()
    for b in range(2):
        for d in range(1, nacross):
            forward(d, b).wait_recv()
            forward(d, b).start()
    for copy in own:
        copy.wait()
    for b in range(2):
        for d in range(nacross):
            slot = 2 * (2 * lax.rem(across + d, nacross) + 1 - core) + b
            remote(
                g.at[slot], g.at[slot], f_send.at[0, b], g_recv.at[slot], (me, sibling)
            ).wait_recv()

    seats.wait()
    first = seat_ref[2 * place]
    second = seat_ref[2 * place + 1]

    def tiles(c, t):
        start = c * chunk + t * (TILE * GROUP)
        return [pl.ds(start + i * TILE, TILE) for i in range(GROUP)]

    for c in range(CHUNKS):
        @pl.loop(0, chunk // (TILE * GROUP))
        def seat(t):
            for rows in tiles(c, t):
                x[0, 0, rows, :] = g[first, rows, :]
                x[0, 1, rows, :] = g[second, rows, :]

    def partial_copy(s, d):
        return remote(
            part.at[s, me], part.at[s, me], p_send.at[s, d], p_recv.at[s, me],
            (lax.rem(me + d, nrow), place),
        )

    def move(s, way, c):
        rows = pl.ds(c * chunk, chunk)
        if way == 0:
            src = r.at[s, jnp.where(has_prev, 0, 1), rows]
            target = lax.rem(place + 1, npair)
        else:
            src = r.at[s, 1, rows]
            target = lax.rem(place + npair - 1, npair)
        return remote(
            src, x.at[s + 1, way, rows], m_send.at[s, way, c], m_recv.at[s, way, c], (me, target)
        )

    def arrived(s, c):
        @pl.when(has_prev)
        def _():
            move(s, 0, c).wait_recv()

        @pl.when(has_next)
        def _():
            move(s, 1, c).wait_recv()

    kept = jnp.where(has_prev, jnp.where(has_next, 2, 1), 0)

    @pl.loop(0, STEPS)
    def step(s):
        sums = tuple(jnp.zeros((TILE, B), jnp.float32) for _ in range(BANDS - 1))
        for c in range(CHUNKS):
            @pl.when(s > 0)
            def _():
                arrived(s - 1, c)

            def add(t, totals):
                for rows in tiles(c, t):
                    products = band_products(x[s, 0, rows, :], x[s, 1, rows, :])
                    totals = tuple(a + b for a, b in zip(totals, products))
                return totals

            sums = lax.fori_loop(0, chunk // (TILE * GROUP), add, sums)
        for k in range(BANDS - 1):
            part[s, me, k:k + 1, :] = jnp.sum(sums[k], axis=0, keepdims=True)
        part[s, me, BANDS - 1:BANDS, :] = jnp.zeros((1, B), jnp.float32)
        for d in range(1, nrow):
            partial_copy(s, d).start()
        for d in range(1, nrow):
            source = lax.rem(me + d, nrow)
            remote(
                part.at[s, source], part.at[s, source], p_send.at[s, d], p_recv.at[s, source],
                (source, place),
            ).wait_recv()
        whole = part[s, 0]
        for k in range(1, nrow):
            whole = whole + part[s, k]
        bands = [jnp.broadcast_to(whole[k:k + 1, :], (TILE, B)) for k in range(BANDS - 1)]
        turns = solve_bands(bands)
        for c in range(CHUNKS):
            @pl.loop(0, chunk // (TILE * GROUP))
            def rotate(t):
                held = tiles(c, t)
                pairs = turn([(x[s, 0, rows, :], x[s, 1, rows, :]) for rows in held], turns)
                for rows, (upper, lower) in zip(held, pairs):
                    r[s, 0, rows, :] = upper
                    r[s, 1, rows, :] = lower
                    x[s + 1, kept, rows, :] = upper

            @pl.when(has_next)
            def _():
                move(s, 0, c).start()

            @pl.when(has_prev)
            def _():
                move(s, 1, c).start()

    for c in range(CHUNKS):
        arrived(STEPS - 1, c)

        @pl.loop(0, chunk // (TILE * GROUP))
        def hand_out(t):
            for rows in tiles(c, t):
                out_ref[rows, 0:B] = x[STEPS, 0, rows, :]
                out_ref[rows, B:2 * B] = x[STEPS, 1, rows, :]

    for b in range(2):
        for d in range(nacross):
            direct(d, b).wait_send()
            if d:
                forward(d, b).wait_send()

    @pl.loop(0, STEPS)
    def drain(s):
        for d in range(1, nrow):
            partial_copy(s, d).wait_send()
        for c in range(CHUNKS):
            @pl.when(has_next)
            def _():
                move(s, 0, c).wait_send()

            @pl.when(has_prev)
            def _():
                move(s, 1, c).wait_send()


def local(nrow, npair, matrix, seating):
    height = matrix.shape[0]
    nacross = npair // 2
    dma = pltpu.SemaphoreType.DMA
    return pl.pallas_call(
        functools.partial(kernel, nrow, npair),
        out_shape=jax.ShapeDtypeStruct(matrix.shape, jnp.float32),
        in_specs=[
            pl.BlockSpec(memory_space=pltpu.HBM),
            pl.BlockSpec(memory_space=pltpu.HBM),
        ],
        out_specs=pl.BlockSpec(memory_space=pltpu.VMEM),
        scratch_shapes=[
            pltpu.SMEM((2 * npair,), jnp.int32),
            pltpu.VMEM((2 * npair, height, B), jnp.float32),
            pltpu.VMEM((STEPS + 1, 3, height, B), jnp.float32),
            pltpu.VMEM((STEPS, 2, height, B), jnp.float32),
            pltpu.VMEM((STEPS, nrow, BANDS, B), jnp.float32),
            dma((nacross, 2)),
            dma((nacross, 2)),
            dma((2 * npair,)),
            dma((STEPS, nrow)),
            dma((STEPS, nrow)),
            dma((STEPS, 2, CHUNKS)),
            dma((STEPS, 2, CHUNKS)),
            dma((2,)),
            dma,
        ],
        compiler_params=pltpu.CompilerParams(
            collective_id=0, has_side_effects=True, vmem_limit_bytes=32 * 1024 * 1024
        ),
    )(seating, matrix)


def solution(mesh):
    sizes = dict(mesh.shape)
    return jax.shard_map(
        functools.partial(local, sizes["row"], sizes["pair"]),
        mesh=mesh, in_specs=(P("row", "pair"), P()), out_specs=P("row", "pair"), check_vma=False,
    )
```

```python
import functools

import jax
import jax.numpy as jnp
from jax import lax
from jax.experimental import pallas as pl
from jax.experimental.pallas import tpu as pltpu
from jax.sharding import PartitionSpec as P

B = 256
STEPS = 4
INNER = 4
TILE = 8
GROUP = 4
CHUNKS = 6
BANDS = 4 * INNER
MESH = pl.DeviceIdType.MESH


def ahead(values, distance):
    shift = (-distance) % B
    return pltpu.roll(values, shift, axis=1) if shift else values


def band_products(upper, lower):
    products = []
    for o in range(INNER):
        u, l = ahead(upper, o), ahead(lower, o)
        products += [upper * u, lower * l, upper * l]
        if o:
            products.append(lower * u)
    return products


def solve_bands(bands):
    uu, ll, ul, lu = {}, {}, {}, {}
    at = 0
    for o in range(INNER):
        uu[o], ll[o], ul[o] = bands[at], bands[at + 1], bands[at + 2]
        at += 3
        if o:
            lu[o] = bands[at]
            at += 1
    turns = []
    for sweep in range(INNER):
        differ = ll[0] - uu[0]
        coupling = ul[0]
        total = uu[0] + ll[0]
        signs = jnp.where(differ >= 0.0, 1.0, -1.0)
        denom = jnp.abs(differ) + jnp.sqrt(
            differ * differ + 4.0 * coupling * coupling + 1e-12 * (total * total)
        )
        tangent = 2.0 * signs * coupling / denom
        c = lax.rsqrt(1.0 + tangent * tangent)
        s = tangent * c
        turns.append((c, s))
        reach = INNER - 1 - sweep
        if reach == 0:
            break
        new_uu, new_ll, new_ul, new_lu = {}, {}, {}, {}
        for o in range(reach + 1):
            cj, sj = ahead(c, o), ahead(s, o)
            a, b, d = uu[o], ul[o], ll[o]
            e = lu[o] if o else ul[0]
            top_u, top_l = c * a - s * e, c * b - s * d
            low_u, low_l = s * a + c * e, s * b + c * d
            new_ul[o] = sj * top_u + cj * top_l
            if o < reach:
                new_uu[o] = cj * top_u - sj * top_l
                new_ll[o] = sj * low_u + cj * low_l
                if o:
                    new_lu[o] = cj * low_u - sj * low_l
        uu = new_uu
        ll = {o: ahead(new_ll[o], 1) for o in new_ll}
        ul = {o: new_ul[o + 1] for o in range(reach)}
        lu = {o: ahead(new_lu[o - 1] if o > 1 else new_ul[0], 1) for o in range(1, reach)}
    return turns


def turn(pairs, turns):
    for k, (c, s) in enumerate(turns):
        pairs = [(c * u - s * l, s * u + c * l) for u, l in pairs]
        distance = 1 if k < INNER - 1 else 1 - INNER
        pairs = [(u, ahead(l, distance)) for u, l in pairs]
    return pairs


def kernel(
    nrow, npair, seating_ref, m_ref, out_ref, seat_ref, g, x, r, part,
    g_send, f_send, g_recv, p_send, p_recv, m_send, m_recv, own_sem, seat_sem,
):
    me = lax.axis_index("row")
    place = lax.axis_index("pair")
    height = m_ref.shape[0]
    chunk = height // CHUNKS
    core = lax.rem(place, 2)
    across = lax.div(place, 2)
    nacross = npair // 2
    sibling = 2 * across + 1 - core
    has_next = place < npair - 1
    has_prev = place > 0

    barrier = pltpu.get_barrier_semaphore()
    for d in range(1, npair):
        pl.semaphore_signal(
            barrier, inc=1, device_id=(me, lax.rem(place + d, npair)), device_id_type=MESH
        )
    for d in range(1, nrow):
        pl.semaphore_signal(
            barrier, inc=1, device_id=(lax.rem(me + d, nrow), place), device_id_type=MESH
        )
    pl.semaphore_wait(barrier, npair + nrow - 2)

    def remote(src, dst, send, recv, device):
        return pltpu.make_async_remote_copy(
            src_ref=src, dst_ref=dst, send_sem=send, recv_sem=recv,
            device_id=device, device_id_type=MESH,
        )

    def columns(b):
        return m_ref.at[:, pl.ds(b * B, B)]

    def direct(d, b):
        target = sibling if d == 0 else 2 * lax.rem(across + d, nacross) + core
        slot = 2 * place + b
        return remote(columns(b), g.at[slot], g_send.at[d, b], g_recv.at[slot], (me, target))

    def forward(d, b):
        slot = 2 * (2 * lax.rem(across + d, nacross) + core) + b
        return remote(g.at[slot], g.at[slot], f_send.at[d, b], g_recv.at[slot], (me, sibling))

    for b in range(2):
        for d in range(1, nacross):
            direct(d, b).start()
    for b in range(2):
        direct(0, b).start()
    seats = pltpu.make_async_copy(seating_ref, seat_ref, seat_sem)
    seats.start()
    own = [
        pltpu.make_async_copy(columns(b), g.at[2 * place + b], own_sem.at[b]) for b in range(2)
    ]
    for copy in own:
        copy.start()
    for b in range(2):
        for d in range(1, nacross):
            forward(d, b).wait_recv()
            forward(d, b).start()
    for copy in own:
        copy.wait()
    for b in range(2):
        for d in range(nacross):
            slot = 2 * (2 * lax.rem(across + d, nacross) + 1 - core) + b
            remote(
                g.at[slot], g.at[slot], f_send.at[0, b], g_recv.at[slot], (me, sibling)
            ).wait_recv()

    seats.wait()
    first = seat_ref[2 * place]
    second = seat_ref[2 * place + 1]

    def tiles(c, t):
        start = c * chunk + t * (TILE * GROUP)
        return [pl.ds(start + i * TILE, TILE) for i in range(GROUP)]

    for c in range(CHUNKS):
        @pl.loop(0, chunk // (TILE * GROUP))
        def seat(t):
            for rows in tiles(c, t):
                x[0, 0, rows, :] = g[first, rows, :]
                x[0, 1, rows, :] = g[second, rows, :]

    def partial_copy(s, d):
        return remote(
            part.at[s, me], part.at[s, me], p_send.at[s, d], p_recv.at[s, me],
            (lax.rem(me + d, nrow), place),
        )

    def move(s, way, c):
        rows = pl.ds(c * chunk, chunk)
        if way == 0:
            src = r.at[s, jnp.where(has_prev, 0, 1), rows]
            target = lax.rem(place + 1, npair)
        else:
            src = r.at[s, 1, rows]
            target = lax.rem(place + npair - 1, npair)
        return remote(
            src, x.at[s + 1, way, rows], m_send.at[s, way, c], m_recv.at[s, way, c], (me, target)
        )

    def arrived(s, c):
        @pl.when(has_prev)
        def _():
            move(s, 0, c).wait_recv()

        @pl.when(has_next)
        def _():
            move(s, 1, c).wait_recv()

    kept = jnp.where(has_prev, jnp.where(has_next, 2, 1), 0)

    @pl.loop(0, STEPS)
    def step(s):
        sums = tuple(jnp.zeros((TILE, B), jnp.float32) for _ in range(BANDS - 1))
        for c in range(CHUNKS):
            @pl.when(s > 0)
            def _():
                arrived(s - 1, c)

            def add(t, totals):
                for rows in tiles(c, t):
                    products = band_products(x[s, 0, rows, :], x[s, 1, rows, :])
                    totals = tuple(a + b for a, b in zip(totals, products))
                return totals

            sums = lax.fori_loop(0, chunk // (TILE * GROUP), add, sums)
        for k in range(BANDS - 1):
            part[s, me, k:k + 1, :] = jnp.sum(sums[k], axis=0, keepdims=True)
        part[s, me, BANDS - 1:BANDS, :] = jnp.zeros((1, B), jnp.float32)
        for d in range(1, nrow):
            partial_copy(s, d).start()
        for d in range(1, nrow):
            source = lax.rem(me + d, nrow)
            remote(
                part.at[s, source], part.at[s, source], p_send.at[s, d], p_recv.at[s, source],
                (source, place),
            ).wait_recv()
        whole = part[s, 0]
        for k in range(1, nrow):
            whole = whole + part[s, k]
        bands = [jnp.broadcast_to(whole[k:k + 1, :], (TILE, B)) for k in range(BANDS - 1)]
        turns = solve_bands(bands)
        for c in range(CHUNKS):
            @pl.loop(0, chunk // (TILE * GROUP))
            def rotate(t):
                held = tiles(c, t)
                pairs = turn([(x[s, 0, rows, :], x[s, 1, rows, :]) for rows in held], turns)
                for rows, (upper, lower) in zip(held, pairs):
                    r[s, 0, rows, :] = upper
                    r[s, 1, rows, :] = lower
                    x[s + 1, kept, rows, :] = upper

            @pl.when(has_next)
            def _():
                move(s, 0, c).start()

            @pl.when(has_prev)
            def _():
                move(s, 1, c).start()

    for c in range(CHUNKS):
        arrived(STEPS - 1, c)

        @pl.loop(0, chunk // (TILE * GROUP))
        def hand_out(t):
            for rows in tiles(c, t):
                out_ref[rows, 0:B] = x[STEPS, 0, rows, :]
                out_ref[rows, B:2 * B] = x[STEPS, 1, rows, :]

    for b in range(2):
        for d in range(nacross):
            direct(d, b).wait_send()
            if d:
                forward(d, b).wait_send()

    @pl.loop(0, STEPS)
    def drain(s):
        for d in range(1, nrow):
            partial_copy(s, d).wait_send()
        for c in range(CHUNKS):
            @pl.when(has_next)
            def _():
                move(s, 0, c).wait_send()

            @pl.when(has_prev)
            def _():
                move(s, 1, c).wait_send()


def local(nrow, npair, matrix, seating):
    height = matrix.shape[0]
    nacross = npair // 2
    dma = pltpu.SemaphoreType.DMA
    return pl.pallas_call(
        functools.partial(kernel, nrow, npair),
        out_shape=jax.ShapeDtypeStruct(matrix.shape, jnp.float32),
        in_specs=[
            pl.BlockSpec(memory_space=pltpu.HBM),
            pl.BlockSpec(memory_space=pltpu.HBM),
        ],
        out_specs=pl.BlockSpec(memory_space=pltpu.VMEM),
        scratch_shapes=[
            pltpu.SMEM((2 * npair,), jnp.int32),
            pltpu.VMEM((2 * npair, height, B), jnp.float32),
            pltpu.VMEM((STEPS + 1, 3, height, B), jnp.float32),
            pltpu.VMEM((STEPS, 2, height, B), jnp.float32),
            pltpu.VMEM((STEPS, nrow, BANDS, B), jnp.float32),
            dma((nacross, 2)),
            dma((nacross, 2)),
            dma((2 * npair,)),
            dma((STEPS, nrow)),
            dma((STEPS, nrow)),
            dma((STEPS, 2, CHUNKS)),
            dma((STEPS, 2, CHUNKS)),
            dma((2,)),
            dma,
        ],
        compiler_params=pltpu.CompilerParams(
            collective_id=0, has_side_effects=True, vmem_limit_bytes=60 * 1024 * 1024
        ),
    )(seating, matrix)


def solution(mesh):
    sizes = dict(mesh.shape)
    return jax.shard_map(
        functools.partial(local, sizes["row"], sizes["pair"]),
        mesh=mesh, in_specs=(P("row", "pair"), P()), out_specs=P("row", "pair"), check_vma=False,
    )
```

```python
import functools

import jax
import jax.numpy as jnp
from jax import lax
from jax.experimental import pallas as pl
from jax.experimental.pallas import tpu as pltpu
from jax.sharding import PartitionSpec as P

B = 256
STEPS = 4
INNER = 4
TILE = 8
GROUP = 4
CHUNKS = 6
BANDS = 4 * INNER
LANES = 128
MESH = pl.DeviceIdType.MESH


def ahead(values, distance):
    shift = (-distance) % B
    return pltpu.roll(values, shift, axis=1) if shift else values


def band_products(upper, lower):
    products = []
    for o in range(INNER):
        u, l = ahead(upper, o), ahead(lower, o)
        products += [upper * u, lower * l, upper * l]
        if o:
            products.append(lower * u)
    return products


def solve_bands(bands):
    uu, ll, ul, lu = {}, {}, {}, {}
    at = 0
    for o in range(INNER):
        uu[o], ll[o], ul[o] = bands[at], bands[at + 1], bands[at + 2]
        at += 3
        if o:
            lu[o] = bands[at]
            at += 1
    turns = []
    for sweep in range(INNER):
        differ = ll[0] - uu[0]
        coupling = ul[0]
        total = uu[0] + ll[0]
        signs = jnp.where(differ >= 0.0, 1.0, -1.0)
        denom = jnp.abs(differ) + jnp.sqrt(
            differ * differ + 4.0 * coupling * coupling + 1e-12 * (total * total)
        )
        tangent = 2.0 * signs * coupling / denom
        c = lax.rsqrt(1.0 + tangent * tangent)
        s = tangent * c
        turns.append((c, s))
        reach = INNER - 1 - sweep
        if reach == 0:
            break
        new_uu, new_ll, new_ul, new_lu = {}, {}, {}, {}
        for o in range(reach + 1):
            cj, sj = ahead(c, o), ahead(s, o)
            a, b, d = uu[o], ul[o], ll[o]
            e = lu[o] if o else ul[0]
            top_u, top_l = c * a - s * e, c * b - s * d
            low_u, low_l = s * a + c * e, s * b + c * d
            new_ul[o] = sj * top_u + cj * top_l
            if o < reach:
                new_uu[o] = cj * top_u - sj * top_l
                new_ll[o] = sj * low_u + cj * low_l
                if o:
                    new_lu[o] = cj * low_u - sj * low_l
        uu = new_uu
        ll = {o: ahead(new_ll[o], 1) for o in new_ll}
        ul = {o: new_ul[o + 1] for o in range(reach)}
        lu = {o: ahead(new_lu[o - 1] if o > 1 else new_ul[0], 1) for o in range(1, reach)}
    return turns


def turn(pairs, turns):
    for k, (c, s) in enumerate(turns):
        pairs = [(c * u - s * l, s * u + c * l) for u, l in pairs]
        distance = 1 if k < INNER - 1 else 1 - INNER
        pairs = [(u, ahead(l, distance)) for u, l in pairs]
    return pairs


def kernel(
    nrow, npair, seating_ref, m_ref, out_ref, seat_ref, g, x, r, part, shares, summed,
    g_send, f_send, g_recv, p_send, p_recv, q_send, q_recv, m_send, m_recv, own_sem, seat_sem,
):
    me = lax.axis_index("row")
    place = lax.axis_index("pair")
    height = m_ref.shape[0]
    chunk = height // CHUNKS
    lines = BANDS * B // LANES // nrow
    core = lax.rem(place, 2)
    across = lax.div(place, 2)
    nacross = npair // 2
    sibling = 2 * across + 1 - core
    has_next = place < npair - 1
    has_prev = place > 0

    barrier = pltpu.get_barrier_semaphore()
    for d in range(1, npair):
        pl.semaphore_signal(
            barrier, inc=1, device_id=(me, lax.rem(place + d, npair)), device_id_type=MESH
        )
    for d in range(1, nrow):
        pl.semaphore_signal(
            barrier, inc=1, device_id=(lax.rem(me + d, nrow), place), device_id_type=MESH
        )
    pl.semaphore_wait(barrier, npair + nrow - 2)

    def remote(src, dst, send, recv, device):
        return pltpu.make_async_remote_copy(
            src_ref=src, dst_ref=dst, send_sem=send, recv_sem=recv,
            device_id=device, device_id_type=MESH,
        )

    def columns(b):
        return m_ref.at[:, pl.ds(b * B, B)]

    def direct(d, b):
        target = sibling if d == 0 else 2 * lax.rem(across + d, nacross) + core
        slot = 2 * place + b
        return remote(columns(b), g.at[slot], g_send.at[d, b], g_recv.at[slot], (me, target))

    def forward(d, b):
        slot = 2 * (2 * lax.rem(across + d, nacross) + core) + b
        return remote(g.at[slot], g.at[slot], f_send.at[d, b], g_recv.at[slot], (me, sibling))

    for b in range(2):
        for d in range(1, nacross):
            direct(d, b).start()
    for b in range(2):
        direct(0, b).start()
    seats = pltpu.make_async_copy(seating_ref, seat_ref, seat_sem)
    seats.start()
    own = [
        pltpu.make_async_copy(columns(b), g.at[2 * place + b], own_sem.at[b]) for b in range(2)
    ]
    for copy in own:
        copy.start()
    for b in range(2):
        for d in range(1, nacross):
            forward(d, b).wait_recv()
            forward(d, b).start()
    for copy in own:
        copy.wait()
    for b in range(2):
        for d in range(nacross):
            slot = 2 * (2 * lax.rem(across + d, nacross) + 1 - core) + b
            remote(
                g.at[slot], g.at[slot], f_send.at[0, b], g_recv.at[slot], (me, sibling)
            ).wait_recv()

    seats.wait()
    first = seat_ref[2 * place]
    second = seat_ref[2 * place + 1]

    def tiles(c, t):
        start = c * chunk + t * (TILE * GROUP)
        return [pl.ds(start + i * TILE, TILE) for i in range(GROUP)]

    for c in range(CHUNKS):
        @pl.loop(0, chunk // (TILE * GROUP))
        def seat(t):
            for rows in tiles(c, t):
                x[0, 0, rows, :] = g[first, rows, :]
                x[0, 1, rows, :] = g[second, rows, :]

    def share_copy(s, d):
        peer = lax.rem(me + d, nrow)
        return remote(
            part.at[s, peer], shares.at[s, d], p_send.at[s, d], p_recv.at[s, d], (peer, place)
        )

    def sum_copy(s, d):
        return remote(
            summed.at[s, me], summed.at[s, me], q_send.at[s, d], q_recv.at[s, me],
            (lax.rem(me + d, nrow), place),
        )

    def sum_from(s, d):
        source = lax.rem(me + d, nrow)
        return remote(
            summed.at[s, source], summed.at[s, source], q_send.at[s, d], q_recv.at[s, source],
            (source, place),
        )

    def move(s, way, c):
        rows = pl.ds(c * chunk, chunk)
        if way == 0:
            src = r.at[s, jnp.where(has_prev, 0, 1), rows]
            target = lax.rem(place + 1, npair)
        else:
            src = r.at[s, 1, rows]
            target = lax.rem(place + npair - 1, npair)
        return remote(
            src, x.at[s + 1, way, rows], m_send.at[s, way, c], m_recv.at[s, way, c], (me, target)
        )

    def arrived(s, c):
        @pl.when(has_prev)
        def _():
            move(s, 0, c).wait_recv()

        @pl.when(has_next)
        def _():
            move(s, 1, c).wait_recv()

    kept = jnp.where(has_prev, jnp.where(has_next, 2, 1), 0)

    @pl.loop(0, STEPS)
    def step(s):
        sums = tuple(jnp.zeros((TILE, B), jnp.float32) for _ in range(BANDS - 1))
        for c in range(CHUNKS):
            @pl.when(s > 0)
            def _():
                arrived(s - 1, c)

            def add(t, totals):
                for rows in tiles(c, t):
                    products = band_products(x[s, 0, rows, :], x[s, 1, rows, :])
                    totals = tuple(a + b for a, b in zip(totals, products))
                return totals

            sums = lax.fori_loop(0, chunk // (TILE * GROUP), add, sums)
        for k in range(BANDS):
            total = jnp.sum(sums[k], axis=0, keepdims=True) if k < BANDS - 1 else jnp.zeros((1, B))
            for h in range(2):
                at = 2 * k + h
                part[s, at // lines, at % lines:at % lines + 1, :] = total[:, h * LANES:(h + 1) * LANES]
        for d in range(1, nrow):
            share_copy(s, d).start()
        whole = part[s, me]
        for d in range(1, nrow):
            share_copy(s, d).wait_recv()
        for d in range(1, nrow):
            whole = whole + shares[s, d]
        summed[s, me] = whole
        for d in range(1, nrow):
            sum_copy(s, d).start()
        for d in range(1, nrow):
            sum_from(s, d).wait_recv()
        bands = []
        for k in range(BANDS - 1):
            halves = []
            for h in range(2):
                at = 2 * k + h
                line = summed[s, at // lines, at % lines:at % lines + 1, :]
                halves.append(jnp.broadcast_to(line, (TILE, LANES)))
            bands.append(jnp.concatenate(halves, axis=1))
        turns = solve_bands(bands)
        for c in range(CHUNKS):
            @pl.loop(0, chunk // (TILE * GROUP))
            def rotate(t):
                held = tiles(c, t)
                pairs = turn([(x[s, 0, rows, :], x[s, 1, rows, :]) for rows in held], turns)
                for rows, (upper, lower) in zip(held, pairs):
                    r[s, 0, rows, :] = upper
                    r[s, 1, rows, :] = lower
                    x[s + 1, kept, rows, :] = upper

            @pl.when(has_next)
            def _():
                move(s, 0, c).start()

            @pl.when(has_prev)
            def _():
                move(s, 1, c).start()

    for c in range(CHUNKS):
        arrived(STEPS - 1, c)

        @pl.loop(0, chunk // (TILE * GROUP))
        def hand_out(t):
            for rows in tiles(c, t):
                out_ref[rows, 0:B] = x[STEPS, 0, rows, :]
                out_ref[rows, B:2 * B] = x[STEPS, 1, rows, :]

    for b in range(2):
        for d in range(nacross):
            direct(d, b).wait_send()
            if d:
                forward(d, b).wait_send()

    @pl.loop(0, STEPS)
    def drain(s):
        for d in range(1, nrow):
            share_copy(s, d).wait_send()
            sum_copy(s, d).wait_send()
        for c in range(CHUNKS):
            @pl.when(has_next)
            def _():
                move(s, 0, c).wait_send()

            @pl.when(has_prev)
            def _():
                move(s, 1, c).wait_send()


def local(nrow, npair, matrix, seating):
    height = matrix.shape[0]
    nacross = npair // 2
    lines = BANDS * B // LANES // nrow
    dma = pltpu.SemaphoreType.DMA
    return pl.pallas_call(
        functools.partial(kernel, nrow, npair),
        out_shape=jax.ShapeDtypeStruct(matrix.shape, jnp.float32),
        in_specs=[
            pl.BlockSpec(memory_space=pltpu.HBM),
            pl.BlockSpec(memory_space=pltpu.HBM),
        ],
        out_specs=pl.BlockSpec(memory_space=pltpu.VMEM),
        scratch_shapes=[
            pltpu.SMEM((2 * npair,), jnp.int32),
            pltpu.VMEM((2 * npair, height, B), jnp.float32),
            pltpu.VMEM((STEPS + 1, 3, height, B), jnp.float32),
            pltpu.VMEM((STEPS, 2, height, B), jnp.float32),
            pltpu.VMEM((STEPS, nrow, lines, LANES), jnp.float32),
            pltpu.VMEM((STEPS, nrow, lines, LANES), jnp.float32),
            pltpu.VMEM((STEPS, nrow, lines, LANES), jnp.float32),
            dma((nacross, 2)),
            dma((nacross, 2)),
            dma((2 * npair,)),
            dma((STEPS, nrow)),
            dma((STEPS, nrow)),
            dma((STEPS, nrow)),
            dma((STEPS, nrow)),
            dma((STEPS, 2, CHUNKS)),
            dma((STEPS, 2, CHUNKS)),
            dma((2,)),
            dma,
        ],
        compiler_params=pltpu.CompilerParams(
            collective_id=0, has_side_effects=True, vmem_limit_bytes=60 * 1024 * 1024
        ),
    )(seating, matrix)


def solution(mesh):
    sizes = dict(mesh.shape)
    return jax.shard_map(
        functools.partial(local, sizes["row"], sizes["pair"]),
        mesh=mesh, in_specs=(P("row", "pair"), P()), out_specs=P("row", "pair"), check_vma=False,
    )
```

```python
import functools

import jax
import jax.numpy as jnp
from jax import lax
from jax.experimental import pallas as pl
from jax.experimental.pallas import tpu as pltpu
from jax.sharding import PartitionSpec as P

B = 256
STEPS = 4
INNER = 4
TILE = 8
GROUP = 4
CHUNKS = 6
PARTS = 3
BANDS = 4 * INNER
MESH = pl.DeviceIdType.MESH


def ahead(values, distance):
    shift = (-distance) % B
    return pltpu.roll(values, shift, axis=1) if shift else values


def band_products(upper, lower):
    products = []
    for o in range(INNER):
        u, l = ahead(upper, o), ahead(lower, o)
        products += [upper * u, lower * l, upper * l]
        if o:
            products.append(lower * u)
    return products


def solve_bands(bands):
    uu, ll, ul, lu = {}, {}, {}, {}
    at = 0
    for o in range(INNER):
        uu[o], ll[o], ul[o] = bands[at], bands[at + 1], bands[at + 2]
        at += 3
        if o:
            lu[o] = bands[at]
            at += 1
    turns = []
    for sweep in range(INNER):
        differ = ll[0] - uu[0]
        coupling = ul[0]
        total = uu[0] + ll[0]
        signs = jnp.where(differ >= 0.0, 1.0, -1.0)
        denom = jnp.abs(differ) + jnp.sqrt(
            differ * differ + 4.0 * coupling * coupling + 1e-12 * (total * total)
        )
        tangent = 2.0 * signs * coupling / denom
        c = lax.rsqrt(1.0 + tangent * tangent)
        s = tangent * c
        turns.append((c, s))
        reach = INNER - 1 - sweep
        if reach == 0:
            break
        new_uu, new_ll, new_ul, new_lu = {}, {}, {}, {}
        for o in range(reach + 1):
            cj, sj = ahead(c, o), ahead(s, o)
            a, b, d = uu[o], ul[o], ll[o]
            e = lu[o] if o else ul[0]
            top_u, top_l = c * a - s * e, c * b - s * d
            low_u, low_l = s * a + c * e, s * b + c * d
            new_ul[o] = sj * top_u + cj * top_l
            if o < reach:
                new_uu[o] = cj * top_u - sj * top_l
                new_ll[o] = sj * low_u + cj * low_l
                if o:
                    new_lu[o] = cj * low_u - sj * low_l
        uu = new_uu
        ll = {o: ahead(new_ll[o], 1) for o in new_ll}
        ul = {o: new_ul[o + 1] for o in range(reach)}
        lu = {o: ahead(new_lu[o - 1] if o > 1 else new_ul[0], 1) for o in range(1, reach)}
    return turns


def turn(pairs, turns):
    for k, (c, s) in enumerate(turns):
        pairs = [(c * u - s * l, s * u + c * l) for u, l in pairs]
        distance = 1 if k < INNER - 1 else 1 - INNER
        pairs = [(u, ahead(l, distance)) for u, l in pairs]
    return pairs


def kernel(
    nrow, npair, seating_ref, m_ref, out_ref, seat_ref, *rest
):
    g, rest = rest[:PARTS], rest[PARTS:]
    (x, r, part, g_send, f_send, g_recv, p_send, p_recv, m_send, m_recv, own_sem, seat_sem) = rest
    me = lax.axis_index("row")
    place = lax.axis_index("pair")
    height = m_ref.shape[0]
    chunk = height // CHUNKS
    core = lax.rem(place, 2)
    across = lax.div(place, 2)
    nacross = npair // 2
    sibling = 2 * across + 1 - core
    has_next = place < npair - 1
    has_prev = place > 0

    barrier = pltpu.get_barrier_semaphore()
    for d in range(1, npair):
        pl.semaphore_signal(
            barrier, inc=1, device_id=(me, lax.rem(place + d, npair)), device_id_type=MESH
        )
    for d in range(1, nrow):
        pl.semaphore_signal(
            barrier, inc=1, device_id=(lax.rem(me + d, nrow), place), device_id_type=MESH
        )
    pl.semaphore_wait(barrier, npair + nrow - 2)

    def remote(src, dst, send, recv, device):
        return pltpu.make_async_remote_copy(
            src_ref=src, dst_ref=dst, send_sem=send, recv_sem=recv,
            device_id=device, device_id_type=MESH,
        )

    part_rows = height // PARTS

    def columns(b, q):
        return m_ref.at[pl.ds(q * part_rows, part_rows), pl.ds(b * B, B)]

    def held(slot, q):
        return g[q].at[slot]

    def direct(d, b, q):
        target = sibling if d == 0 else 2 * lax.rem(across + d, nacross) + core
        slot = 2 * place + b
        return remote(
            columns(b, q), held(slot, q), g_send.at[d, b, q], g_recv.at[slot, q], (me, target)
        )

    def passed_on(d, b, q, owner_core):
        slot = 2 * (2 * lax.rem(across + d, nacross) + owner_core) + b
        return remote(
            held(slot, q), held(slot, q), f_send.at[d, b, q], g_recv.at[slot, q], (me, sibling)
        )

    def own(b, q):
        return pltpu.make_async_copy(columns(b, q), held(2 * place + b, q), own_sem.at[b, q])

    seats = pltpu.make_async_copy(seating_ref, seat_ref, seat_sem)
    seats.start()
    for q in range(PARTS):
        for b in range(2):
            for d in range(1, nacross):
                direct(d, b, q).start()
            direct(0, b, q).start()
            own(b, q).start()
    seats.wait()
    first = seat_ref[2 * place]
    second = seat_ref[2 * place + 1]

    def tiles(c, t):
        start = c * chunk + t * (TILE * GROUP)
        return [pl.ds(start + i * TILE, TILE) for i in range(GROUP)]

    def gathered(q):
        for b in range(2):
            for d in range(1, nacross):
                passed_on(d, b, q, core).wait_recv()
                passed_on(d, b, q, core).start()
        for b in range(2):
            own(b, q).wait()
            for d in range(nacross):
                passed_on(d, b, q, 1 - core).wait_recv()
        each = CHUNKS // PARTS
        for c in range(q * each, (q + 1) * each):
            @pl.loop(0, chunk // (TILE * GROUP))
            def seat(t):
                for rows, within in zip(tiles(c, t), tiles(c - q * each, t)):
                    x[0, 0, rows, :] = g[q][first, within, :]
                    x[0, 1, rows, :] = g[q][second, within, :]

    def peer(d):
        down = nrow - d
        up = d - 1
        return jnp.where(
            2 * me < nrow,
            jnp.where(down <= me, down - 1, down),
            jnp.where(up >= me, up + 1, up),
        )

    def partial_copy(s, d):
        return remote(
            part.at[s, me], part.at[s, me], p_send.at[s, d], p_recv.at[s, me], (peer(d), place)
        )

    def move(s, way, c):
        rows = pl.ds(c * chunk, chunk)
        if way == 0:
            src = r.at[s, jnp.where(has_prev, 0, 1), rows]
            target = lax.rem(place + 1, npair)
        else:
            src = r.at[s, 1, rows]
            target = lax.rem(place + npair - 1, npair)
        return remote(
            src, x.at[s + 1, way, rows], m_send.at[s, way, c], m_recv.at[s, way, c], (me, target)
        )

    def arrived(s, c):
        @pl.when(has_prev)
        def _():
            move(s, 0, c).wait_recv()

        @pl.when(has_next)
        def _():
            move(s, 1, c).wait_recv()

    kept = jnp.where(has_prev, jnp.where(has_next, 2, 1), 0)

    @pl.loop(0, STEPS)
    def step(s):
        sums = tuple(jnp.zeros((TILE, B), jnp.float32) for _ in range(BANDS - 1))
        for c in range(CHUNKS):
            @pl.when(s > 0)
            def _():
                arrived(s - 1, c)

            if c % (CHUNKS // PARTS) == 0:
                @pl.when(s == 0)
                def _():
                    gathered(c // (CHUNKS // PARTS))

            def add(t, totals):
                for rows in tiles(c, t):
                    products = band_products(x[s, 0, rows, :], x[s, 1, rows, :])
                    totals = tuple(a + b for a, b in zip(totals, products))
                return totals

            sums = lax.fori_loop(0, chunk // (TILE * GROUP), add, sums)
        for k in range(BANDS - 1):
            part[s, me, k:k + 1, :] = jnp.sum(sums[k], axis=0, keepdims=True)
        part[s, me, BANDS - 1:BANDS, :] = jnp.zeros((1, B), jnp.float32)
        for d in range(1, nrow):
            partial_copy(s, d).start()
        for d in range(1, nrow):
            source = peer(d)
            remote(
                part.at[s, source], part.at[s, source], p_send.at[s, d], p_recv.at[s, source],
                (source, place),
            ).wait_recv()
        whole = part[s, 0]
        for k in range(1, nrow):
            whole = whole + part[s, k]
        bands = [jnp.broadcast_to(whole[k:k + 1, :], (TILE, B)) for k in range(BANDS - 1)]
        turns = solve_bands(bands)
        for c in range(CHUNKS):
            @pl.loop(0, chunk // (TILE * GROUP))
            def rotate(t):
                group = tiles(c, t)
                pairs = turn([(x[s, 0, rows, :], x[s, 1, rows, :]) for rows in group], turns)
                for rows, (upper, lower) in zip(group, pairs):
                    r[s, 0, rows, :] = upper
                    r[s, 1, rows, :] = lower
                    x[s + 1, kept, rows, :] = upper

            @pl.when(has_next)
            def _():
                move(s, 0, c).start()

            @pl.when(has_prev)
            def _():
                move(s, 1, c).start()

    for c in range(CHUNKS):
        arrived(STEPS - 1, c)

        @pl.loop(0, chunk // (TILE * GROUP))
        def hand_out(t):
            for rows in tiles(c, t):
                out_ref[rows, 0:B] = x[STEPS, 0, rows, :]
                out_ref[rows, B:2 * B] = x[STEPS, 1, rows, :]

    for q in range(PARTS):
        for b in range(2):
            for d in range(nacross):
                direct(d, b, q).wait_send()
                if d:
                    passed_on(d, b, q, core).wait_send()

    @pl.loop(0, STEPS)
    def drain(s):
        for d in range(1, nrow):
            partial_copy(s, d).wait_send()
        for c in range(CHUNKS):
            @pl.when(has_next)
            def _():
                move(s, 0, c).wait_send()

            @pl.when(has_prev)
            def _():
                move(s, 1, c).wait_send()


def local(nrow, npair, matrix, seating):
    height = matrix.shape[0]
    nacross = npair // 2
    dma = pltpu.SemaphoreType.DMA
    return pl.pallas_call(
        functools.partial(kernel, nrow, npair),
        out_shape=jax.ShapeDtypeStruct(matrix.shape, jnp.float32),
        in_specs=[
            pl.BlockSpec(memory_space=pltpu.HBM),
            pl.BlockSpec(memory_space=pltpu.HBM),
        ],
        out_specs=pl.BlockSpec(memory_space=pltpu.VMEM),
        scratch_shapes=[
            pltpu.SMEM((2 * npair,), jnp.int32),
            *[pltpu.VMEM((2 * npair, height // PARTS, B), jnp.float32) for _ in range(PARTS)],
            pltpu.VMEM((STEPS + 1, 3, height, B), jnp.float32),
            pltpu.VMEM((STEPS, 2, height, B), jnp.float32),
            pltpu.VMEM((STEPS, nrow, BANDS, B), jnp.float32),
            dma((nacross, 2, PARTS)),
            dma((nacross, 2, PARTS)),
            dma((2 * npair, PARTS)),
            dma((STEPS, nrow)),
            dma((STEPS, nrow)),
            dma((STEPS, 2, CHUNKS)),
            dma((STEPS, 2, CHUNKS)),
            dma((2, PARTS)),
            dma,
        ],
        compiler_params=pltpu.CompilerParams(
            collective_id=0, has_side_effects=True, vmem_limit_bytes=60 * 1024 * 1024
        ),
    )(seating, matrix)


def solution(mesh):
    sizes = dict(mesh.shape)
    return jax.shard_map(
        functools.partial(local, sizes["row"], sizes["pair"]),
        mesh=mesh, in_specs=(P("row", "pair"), P()), out_specs=P("row", "pair"), check_vma=False,
    )
```

```python
import functools

import jax
import jax.numpy as jnp
from jax import lax
from jax.experimental import pallas as pl
from jax.experimental.pallas import tpu as pltpu
from jax.sharding import PartitionSpec as P

B = 256
STEPS = 4
INNER = 4
TILE = 8
GROUP = 6
CHUNKS = 4
PARTS = 4
BANDS = 4 * INNER
MESH = pl.DeviceIdType.MESH


def ahead(values, distance):
    shift = (-distance) % B
    return pltpu.roll(values, shift, axis=1) if shift else values


def band_products(upper, lower):
    products = []
    for o in range(INNER):
        u, l = ahead(upper, o), ahead(lower, o)
        products += [upper * u, lower * l, upper * l]
        if o:
            products.append(lower * u)
    return products


def solve_bands(bands):
    uu, ll, ul, lu = {}, {}, {}, {}
    at = 0
    for o in range(INNER):
        uu[o], ll[o], ul[o] = bands[at], bands[at + 1], bands[at + 2]
        at += 3
        if o:
            lu[o] = bands[at]
            at += 1
    turns = []
    for sweep in range(INNER):
        differ = ll[0] - uu[0]
        coupling = ul[0]
        total = uu[0] + ll[0]
        signs = jnp.where(differ >= 0.0, 1.0, -1.0)
        denom = jnp.abs(differ) + jnp.sqrt(
            differ * differ + 4.0 * coupling * coupling + 1e-12 * (total * total)
        )
        tangent = 2.0 * signs * coupling / denom
        c = lax.rsqrt(1.0 + tangent * tangent)
        s = tangent * c
        turns.append((c, s))
        reach = INNER - 1 - sweep
        if reach == 0:
            break
        new_uu, new_ll, new_ul, new_lu = {}, {}, {}, {}
        for o in range(reach + 1):
            cj, sj = ahead(c, o), ahead(s, o)
            a, b, d = uu[o], ul[o], ll[o]
            e = lu[o] if o else ul[0]
            top_u, top_l = c * a - s * e, c * b - s * d
            low_u, low_l = s * a + c * e, s * b + c * d
            new_ul[o] = sj * top_u + cj * top_l
            if o < reach:
                new_uu[o] = cj * top_u - sj * top_l
                new_ll[o] = sj * low_u + cj * low_l
                if o:
                    new_lu[o] = cj * low_u - sj * low_l
        uu = new_uu
        ll = {o: ahead(new_ll[o], 1) for o in new_ll}
        ul = {o: new_ul[o + 1] for o in range(reach)}
        lu = {o: ahead(new_lu[o - 1] if o > 1 else new_ul[0], 1) for o in range(1, reach)}
    return turns


def turn(pairs, turns):
    for k, (c, s) in enumerate(turns):
        pairs = [(c * u - s * l, s * u + c * l) for u, l in pairs]
        distance = 1 if k < INNER - 1 else 1 - INNER
        pairs = [(u, ahead(l, distance)) for u, l in pairs]
    return pairs


def kernel(
    nrow, npair, seating_ref, m_ref, out_ref, seat_ref, *rest
):
    g, rest = rest[:PARTS], rest[PARTS:]
    (x, r, part, g_send, f_send, g_recv, p_send, p_recv, m_send, m_recv, own_sem, seat_sem) = rest
    me = lax.axis_index("row")
    place = lax.axis_index("pair")
    height = m_ref.shape[0]
    chunk = height // CHUNKS
    core = lax.rem(place, 2)
    across = lax.div(place, 2)
    nacross = npair // 2
    sibling = 2 * across + 1 - core
    has_next = place < npair - 1
    has_prev = place > 0

    barrier = pltpu.get_barrier_semaphore()
    for d in range(1, npair):
        pl.semaphore_signal(
            barrier, inc=1, device_id=(me, lax.rem(place + d, npair)), device_id_type=MESH
        )
    for d in range(1, nrow):
        pl.semaphore_signal(
            barrier, inc=1, device_id=(lax.rem(me + d, nrow), place), device_id_type=MESH
        )
    pl.semaphore_wait(barrier, npair + nrow - 2)

    def remote(src, dst, send, recv, device):
        return pltpu.make_async_remote_copy(
            src_ref=src, dst_ref=dst, send_sem=send, recv_sem=recv,
            device_id=device, device_id_type=MESH,
        )

    part_rows = height // PARTS

    def columns(b, q):
        return m_ref.at[pl.ds(q * part_rows, part_rows), pl.ds(b * B, B)]

    def held(slot, q):
        return g[q].at[slot]

    def direct(d, b, q):
        target = sibling if d == 0 else 2 * lax.rem(across + d, nacross) + core
        slot = 2 * place + b
        return remote(
            columns(b, q), held(slot, q), g_send.at[d, b, q], g_recv.at[slot, q], (me, target)
        )

    def passed_on(d, b, q, owner_core):
        slot = 2 * (2 * lax.rem(across + d, nacross) + owner_core) + b
        return remote(
            held(slot, q), held(slot, q), f_send.at[d, b, q], g_recv.at[slot, q], (me, sibling)
        )

    def own(b, q):
        return pltpu.make_async_copy(columns(b, q), held(2 * place + b, q), own_sem.at[b, q])

    seats = pltpu.make_async_copy(seating_ref, seat_ref, seat_sem)
    seats.start()
    for q in range(PARTS):
        for b in range(2):
            for d in range(1, nacross):
                direct(d, b, q).start()
            direct(0, b, q).start()
            own(b, q).start()
    seats.wait()
    first = seat_ref[2 * place]
    second = seat_ref[2 * place + 1]

    def tiles(c, t):
        start = c * chunk + t * (TILE * GROUP)
        return [pl.ds(start + i * TILE, TILE) for i in range(GROUP)]

    def gathered(q):
        for b in range(2):
            for d in range(1, nacross):
                passed_on(d, b, q, core).wait_recv()
                passed_on(d, b, q, core).start()
        for b in range(2):
            own(b, q).wait()
            for d in range(nacross):
                passed_on(d, b, q, 1 - core).wait_recv()
        each = CHUNKS // PARTS
        for c in range(q * each, (q + 1) * each):
            @pl.loop(0, chunk // (TILE * GROUP))
            def seat(t):
                for rows, within in zip(tiles(c, t), tiles(c - q * each, t)):
                    x[0, 0, rows, :] = g[q][first, within, :]
                    x[0, 1, rows, :] = g[q][second, within, :]

    def peer(d):
        down = nrow - d
        up = d - 1
        return jnp.where(
            2 * me < nrow,
            jnp.where(down <= me, down - 1, down),
            jnp.where(up >= me, up + 1, up),
        )

    def partial_copy(s, d):
        return remote(
            part.at[s, me], part.at[s, me], p_send.at[s, d], p_recv.at[s, me], (peer(d), place)
        )

    def move(s, way, c):
        rows = pl.ds(c * chunk, chunk)
        if way == 0:
            src = r.at[s, jnp.where(has_prev, 0, 1), rows]
            target = lax.rem(place + 1, npair)
        else:
            src = r.at[s, 1, rows]
            target = lax.rem(place + npair - 1, npair)
        return remote(
            src, x.at[s + 1, way, rows], m_send.at[s, way, c], m_recv.at[s, way, c], (me, target)
        )

    def arrived(s, c):
        @pl.when(has_prev)
        def _():
            move(s, 0, c).wait_recv()

        @pl.when(has_next)
        def _():
            move(s, 1, c).wait_recv()

    kept = jnp.where(has_prev, jnp.where(has_next, 2, 1), 0)

    @pl.loop(0, STEPS)
    def step(s):
        sums = tuple(jnp.zeros((TILE, B), jnp.float32) for _ in range(BANDS - 1))
        for c in range(CHUNKS):
            @pl.when(s > 0)
            def _():
                arrived(s - 1, c)

            if c % (CHUNKS // PARTS) == 0:
                @pl.when(s == 0)
                def _():
                    gathered(c // (CHUNKS // PARTS))

            def add(t, totals):
                for rows in tiles(c, t):
                    products = band_products(x[s, 0, rows, :], x[s, 1, rows, :])
                    totals = tuple(a + b for a, b in zip(totals, products))
                return totals

            sums = lax.fori_loop(0, chunk // (TILE * GROUP), add, sums)
        for k in range(BANDS - 1):
            part[s, me, k:k + 1, :] = jnp.sum(sums[k], axis=0, keepdims=True)
        part[s, me, BANDS - 1:BANDS, :] = jnp.zeros((1, B), jnp.float32)
        for d in range(1, nrow):
            partial_copy(s, d).start()
        for d in range(1, nrow):
            source = peer(d)
            remote(
                part.at[s, source], part.at[s, source], p_send.at[s, d], p_recv.at[s, source],
                (source, place),
            ).wait_recv()
        whole = part[s, 0]
        for k in range(1, nrow):
            whole = whole + part[s, k]
        bands = [jnp.broadcast_to(whole[k:k + 1, :], (TILE, B)) for k in range(BANDS - 1)]
        turns = solve_bands(bands)
        for c in range(CHUNKS):
            @pl.loop(0, chunk // (TILE * GROUP))
            def rotate(t):
                group = tiles(c, t)
                pairs = turn([(x[s, 0, rows, :], x[s, 1, rows, :]) for rows in group], turns)
                for rows, (upper, lower) in zip(group, pairs):
                    r[s, 0, rows, :] = upper
                    r[s, 1, rows, :] = lower
                    x[s + 1, kept, rows, :] = upper

            @pl.when(has_next)
            def _():
                move(s, 0, c).start()

            @pl.when(has_prev)
            def _():
                move(s, 1, c).start()

    for c in range(CHUNKS):
        arrived(STEPS - 1, c)

        @pl.loop(0, chunk // (TILE * GROUP))
        def hand_out(t):
            for rows in tiles(c, t):
                out_ref[rows, 0:B] = x[STEPS, 0, rows, :]
                out_ref[rows, B:2 * B] = x[STEPS, 1, rows, :]

    for q in range(PARTS):
        for b in range(2):
            for d in range(nacross):
                direct(d, b, q).wait_send()
                if d:
                    passed_on(d, b, q, core).wait_send()

    @pl.loop(0, STEPS)
    def drain(s):
        for d in range(1, nrow):
            partial_copy(s, d).wait_send()
        for c in range(CHUNKS):
            @pl.when(has_next)
            def _():
                move(s, 0, c).wait_send()

            @pl.when(has_prev)
            def _():
                move(s, 1, c).wait_send()


def local(nrow, npair, matrix, seating):
    height = matrix.shape[0]
    nacross = npair // 2
    dma = pltpu.SemaphoreType.DMA
    return pl.pallas_call(
        functools.partial(kernel, nrow, npair),
        out_shape=jax.ShapeDtypeStruct(matrix.shape, jnp.float32),
        in_specs=[
            pl.BlockSpec(memory_space=pltpu.HBM),
            pl.BlockSpec(memory_space=pltpu.HBM),
        ],
        out_specs=pl.BlockSpec(memory_space=pltpu.VMEM),
        scratch_shapes=[
            pltpu.SMEM((2 * npair,), jnp.int32),
            *[pltpu.VMEM((2 * npair, height // PARTS, B), jnp.float32) for _ in range(PARTS)],
            pltpu.VMEM((STEPS + 1, 3, height, B), jnp.float32),
            pltpu.VMEM((STEPS, 2, height, B), jnp.float32),
            pltpu.VMEM((STEPS, nrow, BANDS, B), jnp.float32),
            dma((nacross, 2, PARTS)),
            dma((nacross, 2, PARTS)),
            dma((2 * npair, PARTS)),
            dma((STEPS, nrow)),
            dma((STEPS, nrow)),
            dma((STEPS, 2, CHUNKS)),
            dma((STEPS, 2, CHUNKS)),
            dma((2, PARTS)),
            dma,
        ],
        compiler_params=pltpu.CompilerParams(
            collective_id=0, has_side_effects=True, vmem_limit_bytes=60 * 1024 * 1024
        ),
    )(seating, matrix)


def solution(mesh):
    sizes = dict(mesh.shape)
    return jax.shard_map(
        functools.partial(local, sizes["row"], sizes["pair"]),
        mesh=mesh, in_specs=(P("row", "pair"), P()), out_specs=P("row", "pair"), check_vma=False,
    )
```
